256 devices in a mesh: island: 8 (over z_hi, core), fsdp: 32 (over x, y, z_lo).
Axes of the slice: x: 4, y: 4, z: 8 (z_hi: 4, z_lo: 2; z = z_hi * 2 + z_lo), core: 2. Of those that a mesh axis runs over, the one named last changes fastest.
Arguments:
- gate_pre: bfloat16 [8, 16384, 512], P('island', 'fsdp'), may hold values from -6 to 6
- up_val: bfloat16 [8, 16384, 512], P('island', 'fsdp'), may hold values from -6 to 6
- out_grad: bfloat16 [8, 16384, 8192], P('island', 'fsdp'), may hold values from -0.625 to 0.625
- inner_weights: float32 [8, 512, 8192], P('island', 'fsdp'), as said below
- first_moment: float32 [8, 512, 8192], P('island', 'fsdp'), may hold values from -4 to 4
- second_moment: float32 [8, 512, 8192], P('island', 'fsdp'), may hold values from 0.01 to 1
- anchor: float32 [512, 8192], P('fsdp'), may hold values from -0.5 to 0.5
- outer_momentum: float32 [512, 8192], P('fsdp', 'island'), may hold values from -1.5 to 1.5
Outputs:
- first_next: float32 [8, 512, 8192], P('island', 'fsdp')
- second_next: float32 [8, 512, 8192], P('island', 'fsdp')
- momentum_next: float32 [512, 8192], P('fsdp', 'island')
- anchor_next: float32 [512, 8192], P('fsdp')
The draws below stay inside these ranges and needn't reach their ends.
Inputs may be any that keep to these rules, and one draw needn't show every extreme that they name: `inner_weights`: each replica's weights differ from anchor by at most 0.125 in every entry.
All inputs are finite; a program needn't handle non-finite values.
Results may differ from the reference program's by a relative error of at most 0.0042.
Values sent between devices are 32-bit elements; how exact they have to be, the bound alone decides.
A program may use at most 128 MiB of HBM per device.

```python
import math
import jax
import jax.numpy as jnp
from jax import lax

D = 8192
TOK_DEV = 512
STEP = 100
ISLANDS = 8
FFW = 512
TOK_ISL = 16384


def shared_base(key):
    return 0.125 * jnp.clip(jax.random.normal(key, (FFW, D), jnp.float32), -4.0, 4.0)


def draw_anchor(key, part):
    base = shared_base(key)
    return base


def draw_inner_weights(key, part):
    base = shared_base(key)
    key = jax.random.fold_in(key, 12)
    drift = 0.03125 * jnp.clip(jax.random.normal(key, (ISLANDS, FFW, D), jnp.float32), -4.0, 4.0)
    return base[None] + drift


def block_levels(key, extent, cuts, smallest, top_value):
    def one(axis_at, shards_of):
        steps = jax.random.uniform(jax.random.fold_in(jax.random.fold_in(key, 6), axis_at), (shards_of,), jnp.float32, smallest / len(cuts), top_value / len(cuts))
        return jnp.repeat(jnp.exp(steps), extent[axis_at] // shards_of).reshape((-1,) + (1,) * (len(extent) - axis_at - 1))

    gain = one(*cuts[0])
    for cut in cuts[1:]:
        gain = gain * one(*cut)
    return gain


def centred(rng, extent, deviation, limit, cuts=(), kind=jnp.bfloat16):
    drawn = deviation * jax.random.normal(rng, extent, jnp.float32)
    if cuts:
        drawn = drawn * block_levels(rng, extent, cuts, -0.22, 0.18)
    return jnp.clip(drawn, -limit, limit).astype(kind)


def setup_inputs(seed: int = 0) -> dict:
    key_list = jax.random.split(jax.random.key(seed), 9)
    return {
        "gate_pre": centred(key_list[0], (ISLANDS, TOK_ISL, FFW), 1.0, 6.0, ((0, 8), (1, 32))),
        "up_val": centred(key_list[1], (ISLANDS, TOK_ISL, FFW), 1.0, 6.0, ((0, 8), (1, 32))),
        "out_grad": centred(key_list[2], (ISLANDS, TOK_ISL, D), (5 * TOK_ISL ** -0.5), 0.625, ((0, 8), (1, 32))),
        "inner_weights": draw_inner_weights(jax.random.fold_in(key_list[8], 71), 0),
        "first_moment": centred(key_list[4], (ISLANDS, FFW, D), 0.3, 4.0, ((0, 8), (1, 32)), jnp.float32),
        "second_moment": jnp.clip(jnp.exp(math.log(1.0) - 4.6051702 * jax.random.uniform(key_list[5], (ISLANDS, FFW, D), jnp.float32) ** block_levels(key_list[5], (ISLANDS, FFW, D), ((0, 8), (1, 32)), -0.2, 0.2)), 0.01, 1.0),
        "anchor": draw_anchor(jax.random.fold_in(key_list[8], 71), 0),
        "outer_momentum": centred(key_list[7], (FFW, D), 0.1, 1.5, ((0, 32), (1, 8)), jnp.float32),
    }


def island_gradient(operands):
    gate_block, up_block, cotangent = operands
    hidden = (jax.nn.silu(gate_block.astype(jnp.float32)) * up_block.astype(jnp.float32)).astype(jnp.bfloat16)
    hidden = hidden.reshape(TOK_ISL // TOK_DEV, TOK_DEV, FFW)
    cotangent = cotangent.reshape(TOK_ISL // TOK_DEV, TOK_DEV, D)

    def accumulate(total, pieces):
        product = lax.dot_general(pieces[0], pieces[1], (((0,), (0,)), ((), ())), preferred_element_type=jnp.float32)
        rounded = lax.optimization_barrier(product.astype(jnp.bfloat16))
        return (total + rounded.astype(jnp.float32), None)
    total, unused = lax.scan(accumulate, jnp.zeros((FFW, D), jnp.float32), (hidden, cotangent))
    return total

def reference(gate_pre, up_val, out_grad, inner_weights, first_moment, second_moment, anchor, outer_momentum):
    gradient = lax.map(island_gradient, (gate_pre, up_val, out_grad))
    first_next = 0.9 * first_moment + 0.1 * gradient
    second_next = 0.95 * second_moment + 0.05 * gradient * gradient
    first_fix = 1.0 - 0.9 ** STEP
    second_fix = 1.0 - 0.95 ** STEP
    update = first_next / first_fix / (jnp.sqrt(second_next / second_fix) + 1e-08)
    weights_next = inner_weights - 0.05 * (update + 0.4 * inner_weights)
    pseudo = lax.optimization_barrier(jnp.sum(anchor[None] - weights_next, axis=0)) / ISLANDS
    momentum_next = 0.9 * outer_momentum + pseudo
    anchor_next = anchor - 0.7 * (pseudo + 0.9 * momentum_next)
    return (first_next, second_next, momentum_next, anchor_next)
```

```python
import functools

import jax
import jax.numpy as jnp
from jax import lax
from jax.experimental import pallas as pl
from jax.experimental.pallas import tpu as pltpu
from jax.sharding import PartitionSpec as P

MESH = pl.DeviceIdType.MESH
STEP = 100
F32 = jnp.float32
W = 1024
ORDER = [
    (0, 0), (0, 6), (0, 1), (0, 7), (1, 0), (1, 6), (0, 2), (0, 8), (0, 12), (1, 1), (1, 7), (2, 0), (0, 14), (2, 6),
    (0, 3), (1, 2), (1, 8), (1, 12), (2, 1), (3, 6), (2, 7), (3, 0), (0, 13), (1, 3), (0, 9), (2, 8), (3, 1), (4, 0),
    (2, 2), (1, 9), (1, 14), (2, 12), (4, 6), (4, 1), (3, 7), (3, 2), (0, 15), (2, 3), (2, 9), (0, 4), (3, 8), (2, 14),
    (0, 10), (3, 12), (4, 7), (4, 2), (0, 5), (3, 9), (3, 3), (5, 0), (1, 13), (5, 6), (0, 11), (5, 1), (3, 14), (1, 4),
    (1, 10), (6, 0), (4, 8), (4, 12), (4, 3), (1, 5), (1, 11), (4, 9), (1, 15), (5, 7), (2, 13), (5, 2), (4, 14), (5, 8),
    (6, 3), (5, 3), (7, 0), (2, 10), (5, 9), (5, 12), (2, 4), (6, 1), (6, 4), (2, 11), (7, 3), (2, 15), (2, 5), (3, 13),
    (7, 1), (5, 14), (3, 4), (7, 4), (3, 10), (3, 11), (3, 15), (3, 5), (4, 10), (4, 13), (4, 11), (4, 15), (4, 4), (4, 5),
    (5, 10), (5, 13), (5, 11), (5, 15), (5, 4), (5, 5), (6, 6), (6, 5), (6, 7), (6, 2), (7, 6), (7, 5), (7, 7), (7, 2),
]
PER = 13
ISL = 11
N_SEM = 16 * PER + 8 * ISL


def kernel(
    gate, up, og, iw, fm, sm, an, om, fn_o, sn_o, mn_o, an_o,
    gv, uv, ov, iwv, fmv, smv, anv, omv, fnv, snv, mnv, antv,
    hf, hb, T, L1, S1, L2, S2, LZ, CZ, CL1, CS1, CL2, CS2, dep, depc, hz,
    ssem, rsem, lsem, osem,
):
    isl = lax.axis_index("island")
    f = lax.axis_index("fsdp")
    zh, core = isl // 2, isl % 2
    x, y, z = f // 8, (f // 2) % 4, f % 2

    def dev(x, y, z):
        return (isl, (x * 4 + y) * 2 + z)

    xp, xm = dev((x + 1) % 4, y, z), dev((x + 3) % 4, y, z)
    yp, ym = dev(x, (y + 1) % 4, z), dev(x, (y + 3) % 4, z)
    zz = dev(x, y, 1 - z)

    def island(rc, rz):
        return ((zh + rz) % 4) * 2 + (core + rc) % 2

    others = [(1, 0), (0, 1), (0, 2), (0, 3), (1, 1), (1, 2), (1, 3)]

    first = [pltpu.make_async_copy(gate.at[0], gv, lsem.at[0]), pltpu.make_async_copy(up.at[0], uv, lsem.at[1])]
    for c in first:
        c.start()

    def load_unit(u):
        def body(j, _):
            pltpu.make_async_copy(
                og.at[0, :, pl.ds(pl.multiple_of(j * 1024 + u * 128, 128), 128)],
                ov.at[u, :, pl.ds(pl.multiple_of(j * 128, 128), 128)],
                lsem.at[7 + u],
            ).start()
            return 0

        lax.fori_loop(0, 8, body, 0)

    used = []
    for s, i in ORDER:
        if s == 0 and i // 2 not in used:
            used.append(i // 2)
    for u in used:
        load_unit(u)
    state = [
        pltpu.make_async_copy(src, dst, lsem.at[2 + i])
        for i, (src, dst) in enumerate([(iw.at[0], iwv), (fm.at[0], fmv), (sm.at[0], smv), (an, anv), (om, omv)])
    ]
    for c in state:
        c.start()

    barrier = pltpu.get_barrier_semaphore()
    peers = [xp, xm, yp, ym, zz] + [(island(rc, rz), f) for rc, rz in others]
    for d in peers:
        pl.semaphore_signal(barrier, inc=1, device_id=d, device_id_type=MESH)

    for c in first:
        c.wait()

    def silu_rows(t, _):
        rows = pl.ds(pl.multiple_of(t * 128, 128), 128)
        v = gv[rows, :].astype(F32)
        h = v / (1.0 + jnp.exp(-v)) * uv[rows, :].astype(F32)
        hf[:, rows] = h.astype(jnp.bfloat16).astype(F32).T
        return 0

    for t in range(4):
        silu_rows(t, 0)

    def permute(i, _):
        h, kx, ky = i // 16, (i // 4) % 4, i % 4
        base = (((x + kx) % 4) * 4 + (y + ky) % 4) * 2
        a = hf[pl.ds(pl.multiple_of((base + z) * 16 + 8 * h, 8), 8), :]
        b = hf[pl.ds(pl.multiple_of((base + 1 - z) * 16 + 8 * h, 8), 8), :]
        hb[pl.ds(pl.multiple_of(i * 16, 16), 16), :] = jnp.concatenate([a, b], axis=0).astype(jnp.bfloat16)
        return 0

    lax.fori_loop(0, 32, permute, 0)
    pl.semaphore_wait(barrier, len(peers))

    copies = {}

    def send(key, n, src, dst, to):
        c = pltpu.make_async_remote_copy(
            src_ref=src, dst_ref=dst, send_sem=ssem.at[n], recv_sem=rsem.at[n], device_id=to, device_id_type=MESH
        )
        c.start()
        copies[key] = c

    def arrived(*keys):
        for key in keys:
            copies[key].wait_recv()

    def add(dst, *srcs):
        n = dst.shape[0]
        if len(dst.shape) == 2:
            dst[...] = sum([s[...] for s in srcs], dst[...])
            return

        def body(i, _):
            dst[i] = sum([s[i] for s in srcs], dst[i])
            return 0

        lax.fori_loop(0, n, body, 0)

    def matmul(c):
        u, h = c // 2, c % 2

        def body(t, _):
            cols = pl.ds(pl.multiple_of(t * 256, 256), 256)
            r = lax.dot_general(
                hb[256 * h : 256 * h + 256, :], ov[u, :, cols], (((1,), (0,)), ((), ())), preferred_element_type=F32
            )
            T[c, :, :, :, :, cols] = r.astype(jnp.bfloat16).astype(F32).reshape(4, 4, 2, 8, 256)
            return 0

        lax.fori_loop(0, W // 256, body, 0)

    def ring_raw(c, p, blk, one, two, plus, minus):
        base = c * PER + (0 if p == 1 else 6)
        send((c, p, 0), base, blk(2, 0), one(0), plus)
        send((c, p, 1), base + 1, blk(2, 1), one(1), minus)
        send((c, p, 2), base + 2, blk(1, 1), two(0, 1), plus)
        send((c, p, 3), base + 3, blk(3, 0), two(1, 0), minus)

    def ring_mid(c, p, blk, one, two, plus, minus):
        base = c * PER + (0 if p == 1 else 6)
        arrived((c, p, 0))
        add(blk(1, 0), one(0))
        send((c, p, 4), base + 4, blk(1, 0), two(0, 0), plus)
        arrived((c, p, 1))
        add(blk(3, 1), one(1))
        send((c, p, 5), base + 5, blk(3, 1), two(1, 1), minus)

    def ring_end(c, p, blk, one, two, plus, minus):
        arrived(*[(c, p, i) for i in (2, 3, 4, 5)])
        add(blk(0), two(0), two(1))

    def rings(c):
        t = T.at[c]
        two = pl.ds(0, 2), pl.ds(2, 2)
        if c < 12:
            if c < 6:
                b1 = lambda k, half=None: t.at[k] if half is None else t.at[k, two[half]]
                b2 = lambda k, half=None: t.at[0, k] if half is None else t.at[0, k, half]
            else:
                b1 = lambda k, half=None: t.at[:, k] if half is None else t.at[two[half], k]
                b2 = lambda k, half=None: t.at[k, 0] if half is None else t.at[k, 0, half]
            l1 = lambda d, half=None: L1.at[c, d] if half is None else L1.at[c, d, two[half]]
            l2 = lambda d, half=None: L2.at[c, d] if half is None else L2.at[c, d, half]
            s1, s2 = (lambda d: S1.at[c, d]), (lambda d: S2.at[c, d])
        else:
            i = c - 12
            part = pl.ds(0, 512), pl.ds(512, 512)
            if c < 14:
                b1 = lambda k, half=None: t.at[k, :, 0] if half is None else t.at[k, two[half], 0]
                b2 = lambda k, half=None: t.at[0, k, 0] if half is None else t.at[0, k, 0, :, part[half]]
            else:
                b1 = lambda k, half=None: t.at[:, k, 0] if half is None else t.at[two[half], k, 0]
                b2 = lambda k, half=None: t.at[k, 0, 0] if half is None else t.at[k, 0, 0, :, part[half]]
            l1 = lambda d, half=None: CL1.at[i, d] if half is None else CL1.at[i, d, two[half]]
            l2 = lambda d, half=None: CL2.at[i, d] if half is None else CL2.at[i, d, :, part[half]]
            s1, s2 = (lambda d: CS1.at[i, d]), (lambda d: CS2.at[i, d])
        along_x, along_y = (xp, xm), (yp, ym)
        d1, d2 = (along_x, along_y) if c < 6 or 12 <= c < 14 else (along_y, along_x)
        return (c, 1, b1, s1, l1) + d1, (c, 2, b2, s2, l2) + d2

    def update(c):
        u, h = c // 2, c % 2
        rows = pl.ds(8 * h, 8)
        first_fix = 1.0 - 0.9**STEP
        second_fix = 1.0 - 0.95**STEP

        def body(r, _):
            rc, rz = r // 4, r % 4
            j = island(rc, rz)
            cols = pl.ds(pl.multiple_of(j * 1024 + u * 128, 128), 128)
            g = T[c, 0, 0, 0, :, pl.ds(pl.multiple_of(j * 128, 128), 128)]
            first_next = 0.9 * fmv[rows, cols] + 0.1 * g
            second_next = 0.95 * smv[rows, cols] + 0.05 * g * g
            fnv[rows, cols] = first_next
            snv[rows, cols] = second_next
            upd = first_next / first_fix / (jnp.sqrt(second_next / second_fix) + 1e-08)
            w = iwv[rows, cols]
            dep[u, rc, rz, rows, :] = anv[rows, cols] - (w - 0.05 * (upd + 0.4 * w))
            return 0

        lax.fori_loop(0, 8, body, 0)

    updated = [0]
    out_copies = []

    def finish_chunk(c):
        u = c // 2
        if updated[0] == 0:
            for s in state:
                s.wait()
        update(c)
        updated[0] += 1
        done[c] = True
        if done.get(c ^ 1):
            send((u, "core"), 16 * PER + u * ISL, dep.at[u, 1], depc.at[u], (island(1, 0), f))
        if updated[0] == 16:
            for k, (src, dst) in enumerate([(fnv, fn_o.at[0]), (snv, sn_o.at[0])]):
                o = pltpu.make_async_copy(src, dst, osem.at[k])
                o.start()
                out_copies.append(o)

    done = {}
    own = isl * 1024

    def island_one(u):
        arrived((u, "core"))
        add(dep.at[u, 0], depc.at[u])
        for rz in (2, 1, 3):
            send((u, "sum", rz), 16 * PER + u * ISL + rz, dep.at[u, 0, rz], hz.at[u, rz - 1], (island(0, rz), f))

    def island_two(u):
        arrived(*[(u, "sum", rz) for rz in (1, 2, 3)])
        cols = pl.ds(128 * u, 128)
        pseudo = (dep[u, 0, 0] + hz[u, 0] + hz[u, 1] + hz[u, 2]) / 8
        momentum = 0.9 * omv[:, cols] + pseudo
        mnv[:, cols] = momentum
        out = pl.ds(pl.multiple_of(own + u * 128, 128), 128)
        antv[u] = anv[:, out] - 0.7 * (pseudo + 0.9 * momentum)
        for k, (rc, rz) in enumerate([(0, 2), (1, 2), (0, 1), (1, 1), (0, 3), (1, 3), (1, 0)]):
            send((u, "all", k), 16 * PER + u * ISL + 4 + k, antv.at[u], an_o.at[:, out], (island(rc, rz), f))
        o = pltpu.make_async_copy(antv.at[u], an_o.at[:, out], osem.at[3 + u])
        o.start()
        out_copies.append(o)

    for s, i in ORDER:
        if s == 6:
            island_one(i)
            continue
        if s == 7:
            island_two(i)
            continue
        r1, r2 = rings(i)
        if s == 0:
            if i // 2 in used:
                u = i // 2
                used.remove(u)
                pltpu.make_async_copy(og.at[0, :, pl.ds(0, W)], ov.at[u], lsem.at[7 + u]).wait()
            matmul(i)
        if i < 12:
            if s == 0:
                ring_raw(*r1)
            elif s == 1:
                ring_mid(*r1)
            elif s == 2:
                ring_end(*r1)
                ring_raw(*r2)
            elif s == 3:
                ring_mid(*r2)
            elif s == 4:
                ring_end(*r2)
                send((i, "z"), i * PER + 12, T.at[i, 0, 0, 1], LZ.at[i], zz)
            else:
                arrived((i, "z"))
                add(T.at[i, 0, 0, 0], LZ.at[i])
                finish_chunk(i)
        else:
            if s == 0:
                send((i, "z"), i * PER + 12, T.at[i, :, :, 1], CZ.at[i - 12], zz)
            elif s == 1:
                arrived((i, "z"))
                for k in range(4):
                    add(T.at[i, k, :, 0], CZ.at[i - 12, k])
                ring_raw(*r1)
            elif s == 2:
                ring_mid(*r1)
            elif s == 3:
                ring_end(*r1)
                ring_raw(*r2)
            elif s == 4:
                ring_mid(*r2)
            else:
                ring_end(*r2)
                finish_chunk(i)

    o = pltpu.make_async_copy(mnv, mn_o, osem.at[2])
    o.start()
    out_copies.append(o)
    for key, c in copies.items():
        if key[1] == "all":
            c.wait_recv()
    for c in copies.values():
        c.wait_send()
    for o in out_copies:
        o.wait()


def on_device(*args):
    V = pltpu.VMEM
    anyspace = pl.BlockSpec(memory_space=pl.ANY)
    return pl.pallas_call(
        kernel,
        out_shape=(
            jax.ShapeDtypeStruct((1, 16, 8192), F32),
            jax.ShapeDtypeStruct((1, 16, 8192), F32),
            jax.ShapeDtypeStruct((16, 1024), F32),
            jax.ShapeDtypeStruct((16, 8192), F32),
        ),
        in_specs=[anyspace] * 8,
        out_specs=[anyspace] * 4,
        scratch_shapes=[
            V((512, 512), jnp.bfloat16), V((512, 512), jnp.bfloat16), V((8, 512, W), jnp.bfloat16),
            V((16, 8192), F32), V((16, 8192), F32), V((16, 8192), F32), V((16, 8192), F32), V((16, 1024), F32),
            V((16, 8192), F32), V((16, 8192), F32), V((16, 1024), F32), V((8, 16, 128), F32),
            V((512, 512), F32), V((512, 512), jnp.bfloat16), V((16, 4, 4, 2, 8, W), F32),
            V((12, 2, 4, 2, 8, W), F32), V((12, 2, 2, 2, 8, W), F32), V((12, 2, 2, 8, W), F32), V((12, 2, 8, W), F32),
            V((12, 8, W), F32),
            V((4, 4, 4, 8, W), F32), V((4, 2, 4, 8, W), F32), V((4, 2, 2, 8, W), F32), V((4, 2, 8, W), F32),
            V((4, 2, 8, W // 2), F32),
            V((8, 2, 4, 16, 128), F32), V((8, 4, 16, 128), F32), V((8, 3, 16, 128), F32),
            pltpu.SemaphoreType.DMA((N_SEM,)), pltpu.SemaphoreType.DMA((N_SEM,)),
            pltpu.SemaphoreType.DMA((15,)), pltpu.SemaphoreType.DMA((11,)),
        ],
        compiler_params=pltpu.CompilerParams(
            collective_id=0, has_side_effects=True, vmem_limit_bytes=60 * 2**20
        ),
        cost_estimate=pl.CostEstimate(flops=4300000000, bytes_accessed=13000000, transcendentals=400000),
        name="round",
    )(*args)


def solution(mesh):
    rows = P("island", "fsdp", None)
    return jax.shard_map(
        on_device,
        mesh=mesh,
        in_specs=(rows,) * 6 + (P("fsdp", None), P("fsdp", "island")),
        out_specs=(rows, rows, P("fsdp", "island"), P("fsdp", None)),
        check_vma=False,
    )
```

```python
import functools

import jax
import jax.numpy as jnp
from jax import lax
from jax.experimental import pallas as pl
from jax.experimental.pallas import tpu as pltpu
from jax.sharding import PartitionSpec as P

MESH = pl.DeviceIdType.MESH
STEP = 100
F32 = jnp.float32
W = 1024
ORDER = [
    (0, 0), (0, 6), (0, 1), (0, 7), (1, 0), (1, 6), (0, 2), (0, 8), (0, 12), (1, 1), (1, 7), (2, 0), (0, 14), (2, 6),
    (0, 3), (1, 2), (1, 8), (1, 12), (2, 1), (3, 6), (2, 7), (3, 0), (0, 13), (1, 3), (0, 9), (2, 8), (3, 1), (4, 0),
    (2, 2), (1, 9), (1, 14), (2, 12), (4, 6), (4, 1), (3, 7), (3, 2), (0, 15), (2, 3), (2, 9), (0, 4), (3, 8), (2, 14),
    (0, 10), (3, 12), (4, 7), (4, 2), (0, 5), (3, 9), (3, 3), (5, 0), (1, 13), (5, 6), (0, 11), (5, 1), (3, 14), (1, 4),
    (1, 10), (6, 0), (4, 8), (4, 12), (4, 3), (1, 5), (1, 11), (4, 9), (1, 15), (5, 7), (2, 13), (5, 2), (4, 14), (5, 8),
    (6, 3), (5, 3), (7, 0), (2, 10), (5, 9), (5, 12), (2, 4), (6, 1), (6, 4), (2, 11), (7, 3), (2, 15), (2, 5), (3, 13),
    (7, 1), (5, 14), (3, 4), (7, 4), (3, 10), (3, 11), (3, 15), (3, 5), (4, 10), (4, 13), (4, 11), (4, 15), (4, 4), (4, 5),
    (5, 10), (5, 13), (5, 11), (5, 15), (5, 4), (5, 5), (6, 6), (6, 5), (6, 7), (6, 2), (7, 6), (7, 5), (7, 7), (7, 2),
]
PER = 5
N_RECV = 16 * PER + 17
CLASSES = 13

def kernel(
    gate, up, og, iw, fm, sm, an, om, fn_o, sn_o, mn_o, an_o,
    gv, uv, ov, iwv, fmv, smv, anv, omv,
    hb, T, L1, S1, L2, S2, LZ, CZ, CL1, CS1, CL2, CS2, dep, depc, hz,
    ssem, rsem, lsem,
):
    isl = lax.axis_index("island")
    f = lax.axis_index("fsdp")
    zh, core = isl // 2, isl % 2
    x, y, z = f // 8, (f // 2) % 4, f % 2

    def dev(x, y, z):
        return (isl, (x * 4 + y) * 2 + z)

    xp, xm = dev((x + 1) % 4, y, z), dev((x + 3) % 4, y, z)
    yp, ym = dev(x, (y + 1) % 4, z), dev(x, (y + 3) % 4, z)
    zz = dev(x, y, 1 - z)

    def island(rc, rz):
        return ((zh + rz) % 4) * 2 + (core + rc) % 2

    others = [(1, 0), (0, 1), (0, 2), (0, 3), (1, 1), (1, 2), (1, 3)]

    first = [pltpu.make_async_copy(gate.at[0], gv, lsem.at[0]), pltpu.make_async_copy(up.at[0], uv, lsem.at[1])]
    for c in first:
        c.start()

    def load_unit(u):
        def body(j, _):
            pltpu.make_async_copy(
                og.at[0, :, pl.ds(pl.multiple_of(j * 1024 + u * 128, 128), 128)],
                ov.at[u, :, pl.ds(pl.multiple_of(j * 128, 128), 128)],
                lsem.at[7 + u],
            ).start()
            return 0

        lax.fori_loop(0, 8, body, 0)

    used = []
    for s, i in ORDER:
        if s == 0 and i // 2 not in used:
            used.append(i // 2)
    for u in used[:2]:
        load_unit(u)
    state = [
        pltpu.make_async_copy(src, dst, lsem.at[2 + i])
        for i, (src, dst) in enumerate([(iw.at[0], iwv), (fm.at[0], fmv), (sm.at[0], smv), (an, anv), (om, omv)])
    ]
    barrier = pltpu.get_barrier_semaphore()
    peers = [xp, xm, yp, ym, zz] + [(island(rc, rz), f) for rc, rz in others]
    for d in peers:
        pl.semaphore_signal(barrier, inc=1, device_id=d, device_id_type=MESH)

    i = lax.broadcasted_iota(jnp.int32, (512, 512), 0)
    src = ((x + i // 64) % 4) * 128 + ((y + i // 16) % 4) * 32 + ((z + i // 8) % 2) * 16 + (i // 256) * 8 + i % 8
    pick = (src == lax.broadcasted_iota(jnp.int32, (512, 512), 1)).astype(F32).astype(jnp.bfloat16)
    for c in first:
        c.wait()

    for t in range(4):
        rows = slice(128 * t, 128 * t + 128)
        v = gv[rows, :].astype(F32)
        h = (v / (1.0 + jnp.exp(-v)) * uv[rows, :].astype(F32)).astype(jnp.bfloat16)
        hb[:, rows] = lax.dot_general(pick, h, (((1,), (1,)), ((), ())), preferred_element_type=F32).astype(jnp.bfloat16)
    pl.semaphore_wait(barrier, len(peers))

    def remote(n, k, src, dst, to):
        return pltpu.make_async_remote_copy(
            src_ref=src, dst_ref=dst, send_sem=ssem.at[k], recv_sem=rsem.at[n], device_id=to, device_id_type=MESH
        )

    def send(n, k, src, dst, to):
        remote(n, k, src, dst, to).start()

    def arrived(n, whole):
        remote(n, 0, whole, whole, zz).wait_recv()

    def add(dst, *srcs):
        n = dst.shape[0]
        if len(dst.shape) == 2:
            dst[...] = sum([s[...] for s in srcs], dst[...])
            return

        def body(i, _):
            dst[i] = sum([s[i] for s in srcs], dst[i])
            return 0

        lax.fori_loop(0, n, body, 0)

    def matmul(c):
        u, h = c // 2, c % 2

        def body(t, _):
            cols = pl.ds(pl.multiple_of(t * 256, 256), 256)
            r = lax.dot_general(
                hb[256 * h : 256 * h + 256, :], ov[u, :, cols], (((1,), (0,)), ((), ())), preferred_element_type=F32
            )
            T[c, :, :, :, :, cols] = r.astype(jnp.bfloat16).astype(F32).reshape(4, 4, 2, 8, 256)
            return 0

        lax.fori_loop(0, W // 256, body, 0)

    def ring_raw(n, k, blk, one, two, ones, twos, plus, minus):
        send(n, k, blk(2, 0), one(0), plus)
        send(n, k, blk(2, 1), one(1), minus)
        send(n + 1, k + 1, blk(1, 1), two(0, 1), plus)
        send(n + 1, k + 1, blk(3, 0), two(1, 0), minus)

    def ring_mid(n, k, blk, one, two, ones, twos, plus, minus):
        arrived(n, ones)
        add(blk(1, 0), one(0))
        send(n + 1, k + 1, blk(1, 0), two(0, 0), plus)
        add(blk(3, 1), one(1))
        send(n + 1, k + 1, blk(3, 1), two(1, 1), minus)

    def ring_end(n, k, blk, one, two, ones, twos, plus, minus):
        arrived(n + 1, twos)
        add(blk(0), two(0), two(1))

    def rings(c):
        t = T.at[c]
        two = pl.ds(0, 2), pl.ds(2, 2)
        if c < 12:
            if c < 6:
                b1 = lambda k, half=None: t.at[k] if half is None else t.at[k, two[half]]
                b2 = lambda k, half=None: t.at[0, k] if half is None else t.at[0, k, half]
            else:
                b1 = lambda k, half=None: t.at[:, k] if half is None else t.at[two[half], k]
                b2 = lambda k, half=None: t.at[k, 0] if half is None else t.at[k, 0, half]
            l1 = lambda d, half=None: L1.at[c, d] if half is None else L1.at[c, d, two[half]]
            l2 = lambda d, half=None: L2.at[c, d] if half is None else L2.at[c, d, half]
            s1, s2 = (lambda d: S1.at[c, d]), (lambda d: S2.at[c, d])
            w1, w2 = (S1.at[c], L1.at[c]), (S2.at[c], L2.at[c])
            k = 0
        else:
            i = c - 12
            part = pl.ds(0, 512), pl.ds(512, 512)
            if c < 14:
                b1 = lambda k, half=None: t.at[k, :, 0] if half is None else t.at[k, two[half], 0]
                b2 = lambda k, half=None: t.at[0, k, 0] if half is None else t.at[0, k, 0, :, part[half]]
            else:
                b1 = lambda k, half=None: t.at[:, k, 0] if half is None else t.at[two[half], k, 0]
                b2 = lambda k, half=None: t.at[k, 0, 0] if half is None else t.at[k, 0, 0, :, part[half]]
            l1 = lambda d, half=None: CL1.at[i, d] if half is None else CL1.at[i, d, two[half]]
            l2 = lambda d, half=None: CL2.at[i, d] if half is None else CL2.at[i, d, :, part[half]]
            s1, s2 = (lambda d: CS1.at[i, d]), (lambda d: CS2.at[i, d])
            w1, w2 = (CS1.at[i], CL1.at[i]), (CS2.at[i], CL2.at[i])
            k = 5
        along_x, along_y = (xp, xm), (yp, ym)
        d1, d2 = (along_x, along_y) if c < 6 or 12 <= c < 14 else (along_y, along_x)
        n = c * PER
        return (n, k, b1, s1, l1) + w1 + d1, (n + 2, k + 2, b2, s2, l2) + w2 + d2

    def update(c):
        u, h = c // 2, c % 2
        rows = pl.ds(8 * h, 8)
        first_fix = 1.0 - 0.9**STEP
        second_fix = 1.0 - 0.95**STEP

        def body(r, _):
            rc, rz = r // 4, r % 4
            j = island(rc, rz)
            cols = pl.ds(pl.multiple_of(j * 1024 + u * 128, 128), 128)
            g = T[c, 0, 0, 0, :, pl.ds(pl.multiple_of(j * 128, 128), 128)]
            first_next = 0.9 * fmv[rows, cols] + 0.1 * g
            second_next = 0.95 * smv[rows, cols] + 0.05 * g * g
            fn_o[0, rows, cols] = first_next
            sn_o[0, rows, cols] = second_next
            upd = first_next / first_fix / (jnp.sqrt(second_next / second_fix) + 1e-08)
            w = iwv[rows, cols]
            dep[u, rc, rz, rows, :] = anv[rows, cols] - (w - 0.05 * (upd + 0.4 * w))
            return 0

        lax.fori_loop(0, 8, body, 0)

    updated = [0]

    def finish_chunk(c):
        u = c // 2
        if updated[0] == 0:
            for s in state:
                s.wait()
        update(c)
        updated[0] += 1
        done[c] = True
        if done.get(c ^ 1):
            send(16 * PER + 2 * u, 10, dep.at[u, 1], depc.at[u], (island(1, 0), f))

    done = {}
    own = isl * 1024

    def island_one(u):
        arrived(16 * PER + 2 * u, depc.at[u])
        add(dep.at[u, 0], depc.at[u])
        for rz in (2, 1, 3):
            send(16 * PER + 2 * u + 1, 11, dep.at[u, 0, rz], hz.at[u, rz - 1], (island(0, rz), f))

    def island_two(u):
        arrived(16 * PER + 2 * u + 1, hz.at[u])
        cols = pl.ds(128 * u, 128)
        pseudo = (dep[u, 0, 0] + hz[u, 0] + hz[u, 1] + hz[u, 2]) / 8
        momentum = 0.9 * omv[:, cols] + pseudo
        mn_o[:, cols] = momentum
        out = pl.ds(pl.multiple_of(own + u * 128, 128), 128)
        an_o[:, out] = anv[:, out] - 0.7 * (pseudo + 0.9 * momentum)
        for rc, rz in [(0, 2), (1, 2), (0, 1), (1, 1), (0, 3), (1, 3), (1, 0)]:
            send(N_RECV - 1, 12, an_o.at[:, out], an_o.at[:, out], (island(rc, rz), f))

    for s, i in ORDER:
        if s == 6:
            island_one(i)
            continue
        if s == 7:
            island_two(i)
            continue
        r1, r2 = rings(i)
        if s == 0:
            if i // 2 in used:
                u = i // 2
                used.remove(u)
                if len(used) > 1:
                    load_unit(used[1])
                if len(used) == 4:
                    for c in state:
                        c.start()
                pltpu.make_async_copy(og.at[0, :, pl.ds(0, W)], ov.at[u], lsem.at[7 + u]).wait()
            matmul(i)
        if i < 12:
            if s == 0:
                ring_raw(*r1)
            elif s == 1:
                ring_mid(*r1)
            elif s == 2:
                ring_end(*r1)
                ring_raw(*r2)
            elif s == 3:
                ring_mid(*r2)
            elif s == 4:
                ring_end(*r2)
                send(i * PER + 4, 4, T.at[i, 0, 0, 1], LZ.at[i], zz)
            else:
                arrived(i * PER + 4, LZ.at[i])
                add(T.at[i, 0, 0, 0], LZ.at[i])
                finish_chunk(i)
        else:
            if s == 0:
                send(i * PER + 4, 9, T.at[i, :, :, 1], CZ.at[i - 12], zz)
            elif s == 1:
                arrived(i * PER + 4, CZ.at[i - 12])
                for k in range(4):
                    add(T.at[i, k, :, 0], CZ.at[i - 12, k])
                ring_raw(*r1)
            elif s == 2:
                ring_mid(*r1)
            elif s == 3:
                ring_end(*r1)
                ring_raw(*r2)
            elif s == 4:
                ring_mid(*r2)
            else:
                ring_end(*r2)
                finish_chunk(i)

    results = an_o.at[:, pl.ds(0, 7 * 1024)]
    arrived(N_RECV - 1, results)
    for k, whole in enumerate([S1, L1, S2, L2, LZ, CS1, CL1, CS2, CL2, CZ, depc, hz, results]):
        remote(0, k, whole, whole, zz).wait_send()


def hand_on(a, b, c, d, a_o, b_o, c_o, d_o, sem):
    copies = [pltpu.make_async_copy(p, o, sem.at[i]) for i, (p, o) in enumerate([(a, a_o), (b, b_o), (c, c_o), (d, d_o)])]
    for c in copies:
        c.start()
    for c in copies:
        c.wait()


def on_device(*args):
    V = pltpu.VMEM
    anyspace = pl.BlockSpec(memory_space=pl.ANY)
    shapes = tuple(jax.ShapeDtypeStruct(s, F32) for s in [(1, 16, 8192), (1, 16, 8192), (16, 1024), (16, 8192)])
    outs = pl.pallas_call(
        kernel,
        out_shape=tuple(V(s.shape, F32) for s in shapes),
        in_specs=[anyspace] * 8,
        out_specs=[pl.BlockSpec(memory_space=V)] * 4,
        scratch_shapes=[
            V((512, 512), jnp.bfloat16), V((512, 512), jnp.bfloat16), V((8, 512, W), jnp.bfloat16),
            V((16, 8192), F32), V((16, 8192), F32), V((16, 8192), F32), V((16, 8192), F32), V((16, 1024), F32),
            V((512, 512), jnp.bfloat16), V((16, 4, 4, 2, 8, W), F32),
            V((12, 2, 4, 2, 8, W), F32), V((12, 2, 2, 2, 8, W), F32), V((12, 2, 2, 8, W), F32), V((12, 2, 8, W), F32),
            V((12, 8, W), F32),
            V((4, 4, 4, 8, W), F32), V((4, 2, 4, 8, W), F32), V((4, 2, 2, 8, W), F32), V((4, 2, 8, W), F32),
            V((4, 2, 8, W // 2), F32),
            V((8, 2, 4, 16, 128), F32), V((8, 4, 16, 128), F32), V((8, 3, 16, 128), F32),
            pltpu.SemaphoreType.DMA((CLASSES,)), pltpu.SemaphoreType.DMA((N_RECV,)),
            pltpu.SemaphoreType.DMA((15,)),
        ],
        compiler_params=pltpu.CompilerParams(
            collective_id=0, has_side_effects=True, vmem_limit_bytes=58 * 2**20
        ),
        cost_estimate=pl.CostEstimate(flops=4300000000, bytes_accessed=13000000, transcendentals=400000),
        name="round",
    )(*args)
    return pl.pallas_call(
        hand_on,
        out_shape=shapes,
        in_specs=[pl.BlockSpec(memory_space=V)] * 4,
        out_specs=[anyspace] * 4,
        scratch_shapes=[pltpu.SemaphoreType.DMA((4,))],
        name="hand_on",
    )(*[pltpu.with_memory_space_constraint(o, V) for o in outs])


def solution(mesh):
    rows = P("island", "fsdp", None)
    return jax.shard_map(
        on_device,
        mesh=mesh,
        in_specs=(rows,) * 6 + (P("fsdp", None), P("fsdp", "island")),
        out_specs=(rows, rows, P("fsdp", "island"), P("fsdp", None)),
        check_vma=False,
    )
```

```python
import functools

import jax
import jax.numpy as jnp
from jax import lax
from jax.experimental import pallas as pl
from jax.experimental.pallas import tpu as pltpu
from jax.sharding import PartitionSpec as P

MESH = pl.DeviceIdType.MESH
STEP = 100
F32 = jnp.float32
W = 1024
ORDER = [
    (0, 2), (0, 8), (0, 15), (0, 9), (0, 3), (0, 0), (1, 2), (0, 13), (1, 8), (0, 11), (1, 3), (1, 9), (1, 15),
    (1, 0), (0, 12), (2, 8), (1, 11), (2, 2), (2, 3), (2, 9), (1, 13), (2, 15), (2, 0), (3, 8), (0, 14), (0, 7),
    (3, 9), (0, 5), (2, 11), (2, 13), (3, 2), (3, 3), (4, 8), (0, 10), (4, 9), (3, 15), (0, 1), (3, 0), (1, 5),
    (1, 12), (1, 7), (3, 11), (3, 13), (4, 2), (4, 15), (4, 3), (0, 6), (0, 4), (1, 1), (1, 10), (1, 14), (5, 8),
    (4, 0), (5, 9), (5, 2), (5, 3), (6, 0), (2, 5), (6, 1), (5, 0), (2, 7), (6, 2), (4, 13), (2, 12), (6, 9), (4, 11),
    (5, 15), (1, 6), (7, 0), (6, 6), (1, 4), (5, 11), (7, 1), (7, 2), (7, 9), (6, 8), (2, 10), (8, 0), (2, 14),
    (2, 1), (3, 7), (7, 6), (3, 5), (5, 13), (8, 9), (3, 12), (7, 8), (6, 4), (2, 6), (2, 4), (3, 10), (3, 14),
    (3, 1), (8, 8), (4, 7), (7, 4), (3, 6), (4, 12), (5, 5), (3, 4), (4, 14), (5, 10), (6, 14), (5, 7), (4, 6),
    (5, 12), (6, 7), (5, 1), (6, 12), (5, 14), (5, 4), (6, 3), (6, 10), (5, 6), (6, 5), (6, 13), (7, 14), (6, 11),
    (7, 7), (7, 12), (7, 3), (7, 10), (7, 5), (7, 13), (8, 14), (7, 11), (8, 7), (8, 12), (8, 3), (8, 10), (8, 5),
    (8, 13),
]
GROUPS = [(4, None), (1, 0), (1, 1), (6, 0), (6, 1), (7, 0), (7, 1), (5, 0), (5, 1), (0, 0), (0, 1), (3, 0), (3, 1), (2, 0), (2, 1)]
DIRECT = [2, 4, 11]
SLANTED = [1, 4, 5, 10]
GATHER = [1, 6]
PER = 5
N_RECV = 16 * PER + 3 * len(GROUPS) + 1
CLASSES = 16

def kernel(
    gate, up, og, iw, fm, sm, an, om, fn_o, sn_o, mn_o, an_o,
    gv, uv, ov, iwv, fmv, smv, anv, omv,
    hb, T, L1, S1, L2, S2, LZ, CZ, CL1, CS1, CL2, CS2, dep, depc, hz, gz, omr,
    ssem, rsem, lsem,
):
    isl = lax.axis_index("island")
    f = lax.axis_index("fsdp")
    zh, core = isl // 2, isl % 2
    x, y, z = f // 8, (f // 2) % 4, f % 2

    def dev(x, y, z):
        return (isl, (x * 4 + y) * 2 + z)

    xp, xm = dev((x + 1) % 4, y, z), dev((x + 3) % 4, y, z)
    yp, ym = dev(x, (y + 1) % 4, z), dev(x, (y + 3) % 4, z)
    zz = dev(x, y, 1 - z)
    xpz, xmz = dev((x + 1) % 4, y, 1 - z), dev((x + 3) % 4, y, 1 - z)
    ypz, ymz = dev(x, (y + 1) % 4, 1 - z), dev(x, (y + 3) % 4, 1 - z)

    def island(rc, rz):
        return ((zh + rz) % 4) * 2 + (core + rc) % 2

    others = [(1, 0), (0, 1), (0, 2), (0, 3), (1, 1), (1, 2), (1, 3)]

    first = [pltpu.make_async_copy(gate.at[0], gv, lsem.at[0]), pltpu.make_async_copy(up.at[0], uv, lsem.at[1])]
    for c in first:
        c.start()

    def load_unit(u):
        def body(j, _):
            pltpu.make_async_copy(
                og.at[0, :, pl.ds(pl.multiple_of(j * 1024 + u * 128, 128), 128)],
                ov.at[u, :, pl.ds(pl.multiple_of(j * 128, 128), 128)],
                lsem.at[7 + u],
            ).start()
            return 0

        lax.fori_loop(0, 8, body, 0)

    used = []
    for s, i in ORDER:
        if s == 0 and i // 2 not in used:
            used.append(i // 2)
    for u in used[:2]:
        load_unit(u)
    state = [
        pltpu.make_async_copy(src, dst, lsem.at[2 + i])
        for i, (src, dst) in enumerate([(iw.at[0], iwv), (fm.at[0], fmv), (sm.at[0], smv), (an, anv), (om, omv)])
    ]
    barrier = pltpu.get_barrier_semaphore()
    peers = [xp, xm, yp, ym, zz]
    if any(c < 6 for c in SLANTED):
        peers += [ypz, ymz]
    if any(6 <= c < 12 for c in SLANTED):
        peers += [xpz, xmz]
    peers += [(island(rc, rz), f) for rc, rz in others]
    for d in peers:
        pl.semaphore_signal(barrier, inc=1, device_id=d, device_id_type=MESH)

    i = lax.broadcasted_iota(jnp.int32, (512, 512), 0)
    src = ((x + i // 64) % 4) * 128 + ((y + i // 16) % 4) * 32 + ((z + i // 8) % 2) * 16 + (i // 256) * 8 + i % 8
    pick = (src == lax.broadcasted_iota(jnp.int32, (512, 512), 1)).astype(F32).astype(jnp.bfloat16)
    for c in first:
        c.wait()

    for t in range(4):
        rows = slice(128 * t, 128 * t + 128)
        v = gv[rows, :].astype(F32)
        h = (v / (1.0 + jnp.exp(-v)) * uv[rows, :].astype(F32)).astype(jnp.bfloat16)
        hb[:, rows] = lax.dot_general(pick, h, (((1,), (1,)), ((), ())), preferred_element_type=F32).astype(jnp.bfloat16)
    pl.semaphore_wait(barrier, len(peers))

    def remote(n, k, src, dst, to):
        return pltpu.make_async_remote_copy(
            src_ref=src, dst_ref=dst, send_sem=ssem.at[k], recv_sem=rsem.at[n], device_id=to, device_id_type=MESH
        )

    def send(n, k, src, dst, to):
        remote(n, k, src, dst, to).start()

    def arrived(n, whole):
        remote(n, 0, whole, whole, zz).wait_recv()

    def add(dst, *srcs):
        n = dst.shape[0]
        if len(dst.shape) == 2:
            dst[...] = sum([s[...] for s in srcs], dst[...])
            return

        def body(i, _):
            dst[i] = sum([s[i] for s in srcs], dst[i])
            return 0

        lax.fori_loop(0, n, body, 0)

    def matmul(c):
        u, h = c // 2, c % 2

        def body(t, _):
            cols = pl.ds(pl.multiple_of(t * 256, 256), 256)
            r = lax.dot_general(
                hb[256 * h : 256 * h + 256, :], ov[u, :, cols], (((1,), (0,)), ((), ())), preferred_element_type=F32
            )
            T[c, :, :, :, :, cols] = r.astype(jnp.bfloat16).astype(F32).reshape(4, 4, 2, 8, 256)
            return 0

        lax.fori_loop(0, W // 256, body, 0)

    def ring_raw(n, k, blk, one, two, ones, twos, plus, minus, plus1, minus1):
        send(n, k, blk(2, 0), one(0), plus)
        send(n, k, blk(2, 1), one(1), minus)
        send(n + 1, k + 1, blk(1, 1), two(0, 1), plus1)
        send(n + 1, k + 1, blk(3, 0), two(1, 0), minus)

    def ring_mid(n, k, blk, one, two, ones, twos, plus, minus, plus1, minus1):
        arrived(n, ones)
        add(blk(1, 0), one(0))
        send(n + 1, k + 1, blk(1, 0), two(0, 0), plus)
        add(blk(3, 1), one(1))
        send(n + 1, k + 1, blk(3, 1), two(1, 1), minus1)

    def ring_end(n, k, blk, one, two, ones, twos, plus, minus, plus1, minus1):
        arrived(n + 1, twos)
        add(blk(0), two(0), two(1))

    def rings(c):
        t = T.at[c]
        two = pl.ds(0, 2), pl.ds(2, 2)
        if c < 12:
            if c < 6:
                b1 = lambda k, half=None: t.at[k] if half is None else t.at[k, two[half]]
                b2 = lambda k, half=None: t.at[0, k] if half is None else t.at[0, k, half]
            else:
                b1 = lambda k, half=None: t.at[:, k] if half is None else t.at[two[half], k]
                b2 = lambda k, half=None: t.at[k, 0] if half is None else t.at[k, 0, half]
            l1 = lambda d, half=None: L1.at[c, d] if half is None else L1.at[c, d, two[half]]
            l2 = lambda d, half=None: L2.at[c, d] if half is None else L2.at[c, d, half]
            s1, s2 = (lambda d: S1.at[c, d]), (lambda d: S2.at[c, d])
            w1, w2 = (S1.at[c], L1.at[c]), (S2.at[c], L2.at[c])
            k = 0
        else:
            i = c - 12
            part = pl.ds(0, 512), pl.ds(512, 512)
            if c < 14:
                b1 = lambda k, half=None: t.at[k, :, 0] if half is None else t.at[k, two[half], 0]
                b2 = lambda k, half=None: t.at[0, k, 0] if half is None else t.at[0, k, 0, :, part[half]]
            else:
                b1 = lambda k, half=None: t.at[:, k, 0] if half is None else t.at[two[half], k, 0]
                b2 = lambda k, half=None: t.at[k, 0, 0] if half is None else t.at[k, 0, 0, :, part[half]]
            l1 = lambda d, half=None: CL1.at[i, d] if half is None else CL1.at[i, d, two[half]]
            l2 = lambda d, half=None: CL2.at[i, d] if half is None else CL2.at[i, d, :, part[half]]
            s1, s2 = (lambda d: CS1.at[i, d]), (lambda d: CS2.at[i, d])
            w1, w2 = (CS1.at[i], CL1.at[i]), (CS2.at[i], CL2.at[i])
            k = 5
        along_x, along_y = (xp, xm), (yp, ym)
        d1, d2 = (along_x, along_y) if c < 6 or 12 <= c < 14 else (along_y, along_x)
        n = c * PER
        e2 = d2
        if c in SLANTED:
            e2 = (ypz, ymz) if c < 6 else (xpz, xmz)
        return (n, k, b1, s1, l1) + w1 + d1 + d1, (n + 2, k + 2, b2, s2, l2) + w2 + d2 + e2

    def update(c):
        u, h = c // 2, c % 2
        rows = pl.ds(8 * h, 8)
        first_fix = 1.0 - 0.9**STEP
        second_fix = 1.0 - 0.95**STEP

        def body(r, _):
            rc, rz = r // 4, r % 4
            j = island(rc, rz)
            cols = pl.ds(pl.multiple_of(j * 1024 + u * 128, 128), 128)
            g = T[c, 0, 0, 0, :, pl.ds(pl.multiple_of(j * 128, 128), 128)]
            first_next = 0.9 * fmv[rows, cols] + 0.1 * g
            second_next = 0.95 * smv[rows, cols] + 0.05 * g * g
            fn_o[0, rows, cols] = first_next
            sn_o[0, rows, cols] = second_next
            upd = first_next / first_fix / (jnp.sqrt(second_next / second_fix) + 1e-08)
            w = iwv[rows, cols]
            dep[u, rc, rz, rows, :] = anv[rows, cols] - (w - 0.05 * (upd + 0.4 * w))
            return 0

        lax.fori_loop(0, 8, body, 0)

    updated = [0]

    def finish_chunk(c):
        u = c // 2
        if updated[0] == 0:
            for s in state:
                s.wait()
            for k, g in enumerate(GATHER):
                u, rows, n = group(g)
                for rz in (2, 1, 3):
                    send(n + 2, 14, omv.at[rows, pl.ds(128 * u, 128)], omr.at[k, rz - 1], (island(0, rz), f))
        update(c)
        updated[0] += 1
        done.add(c)
        for g, (u, h) in enumerate(GROUPS):
            if c // 2 == u and (h == c % 2 or h is None and c ^ 1 in done):
                u, rows, n = group(g)
                send(n, 10, dep.at[u, 1, :, rows], depc.at[u, :, rows], (island(1, 0), f))

    done = set()
    own = isl * 1024

    def group(g):
        u, h = GROUPS[g]
        return u, pl.ds(0, 16) if h is None else pl.ds(8 * h, 8), 16 * PER + 3 * g

    def island_one(g):
        u, rows, n = group(g)
        arrived(n, depc.at[u, :, rows])
        add(dep.at[u, 0, :, rows], depc.at[u, :, rows])
        if g in GATHER:
            for rz in (2, 1, 3):
                send(n + 1, 13, dep.at[u, 0, :, rows], gz.at[GATHER.index(g), rz - 1], (island(0, rz), f))
            return
        for rz in (2, 1, 3):
            send(n + 1, 11, dep.at[u, 0, rz, rows], hz.at[u, rz - 1, rows], (island(0, rz), f))

    def gathered(g):
        u, rows, n = group(g)
        k = GATHER.index(g)
        arrived(n + 2, omr.at[k])
        arrived(n + 1, gz.at[k])

        def result(r, old):
            pseudo = ((dep[u, 0, r, rows] + gz[k, 1, (r + 2) % 4]) + (gz[k, 0, (r + 1) % 4] + gz[k, 2, (r + 3) % 4])) / 8
            momentum = 0.9 * old + pseudo
            out = pl.ds(pl.multiple_of(island(0, r) * 1024 + u * 128, 128), 128)
            an_o[rows, out] = anv[rows, out] - 0.7 * (pseudo + 0.9 * momentum)
            send(N_RECV - 1, 15, an_o.at[rows, out], an_o.at[rows, out], (island(1, 0), f))
            return momentum

        cols = pl.ds(128 * u, 128)
        mn_o[rows, cols] = result(0, omv[rows, cols])
        for r in (1, 2, 3):
            result(r, omr[k, 3 - r])

    def island_two(g):
        if g in GATHER:
            gathered(g)
            return
        u, rows, n = group(g)
        arrived(n + 1, hz.at[u, :, rows])
        cols = pl.ds(128 * u, 128)
        pseudo = (dep[u, 0, 0, rows] + hz[u, 0, rows] + hz[u, 1, rows] + hz[u, 2, rows]) / 8
        momentum = 0.9 * omv[rows, cols] + pseudo
        mn_o[rows, cols] = momentum
        out = pl.ds(pl.multiple_of(own + u * 128, 128), 128)
        an_o[rows, out] = anv[rows, out] - 0.7 * (pseudo + 0.9 * momentum)
        res = an_o.at[rows, out]
        for rz in (2, 1, 3):
            send(n + 2, 12, res, res, (island(0, rz), f))
            if g in DIRECT:
                send(N_RECV - 1, 12, res, res, (island(1, rz), f))
        send(N_RECV - 1, 12, res, res, (island(1, 0), f))

    def island_three(g):
        u, rows, n = group(g)
        arrived(n + 2, an_o.at[rows, pl.ds(0, 3 * 128)])
        if g not in DIRECT:
            for rz in (1, 2, 3):
                out = pl.ds(pl.multiple_of(island(0, rz) * 1024 + u * 128, 128), 128)
                send(N_RECV - 1, 12, an_o.at[rows, out], an_o.at[rows, out], (island(1, 0), f))

    for s, i in ORDER:
        if s == 6:
            island_one(i)
            continue
        if s == 7:
            island_two(i)
            continue
        if s == 8:
            island_three(i)
            continue
        r1, r2 = rings(i)
        if s == 0:
            if i // 2 in used:
                u = i // 2
                used.remove(u)
                if len(used) > 1:
                    load_unit(used[1])
                if len(used) == 4:
                    for c in state:
                        c.start()
                pltpu.make_async_copy(og.at[0, :, pl.ds(0, W)], ov.at[u], lsem.at[7 + u]).wait()
            matmul(i)
        if i < 12:
            if s == 0:
                ring_raw(*r1)
            elif s == 1:
                ring_mid(*r1)
            elif s == 2:
                ring_end(*r1)
                ring_raw(*r2)
                if i in SLANTED:
                    send(i * PER + 4, 4, T.at[i, 0, 0, 1], LZ.at[i], zz)
            elif s == 3:
                ring_mid(*r2)
            elif s == 4:
                ring_end(*r2)
                send(i * PER + 4, 4, T.at[i, 0, 0, 1], LZ.at[i], zz)
            else:
                arrived(i * PER + 4, LZ.at[i])
                more = []
                if i in SLANTED:
                    arrived(i * PER + 3, L2.at[i])
                    more = [L2.at[i, d, k] for d in (0, 1) for k in (0, 1)]
                add(T.at[i, 0, 0, 0], LZ.at[i], *more)
                finish_chunk(i)
        else:
            if s == 0:
                send(i * PER + 4, 9, T.at[i, :, :, 1], CZ.at[i - 12], zz)
            elif s == 1:
                arrived(i * PER + 4, CZ.at[i - 12])
                for k in range(4):
                    add(T.at[i, k, :, 0], CZ.at[i - 12, k])
                ring_raw(*r1)
            elif s == 2:
                ring_mid(*r1)
            elif s == 3:
                ring_end(*r1)
                ring_raw(*r2)
            elif s == 4:
                ring_mid(*r2)
            else:
                ring_end(*r2)
                finish_chunk(i)

    for g in DIRECT:
        island_three(g)
    arrived(N_RECV - 1, an_o.at[:, pl.ds(0, 4 * 1024)])
    plain = 16 - len(GATHER)
    for k, whole in [
        (0, S1), (1, L1), (2, S2), (3, L2), (4, LZ), (5, CS1), (6, CL1), (7, CS2), (8, CL2), (9, CZ), (10, depc),
        (11, hz.at[pl.ds(0, plain // 2)]), (12, an_o.at[:, pl.ds(0, 7 * plain // 2 * 128)]),
    ]:
        remote(0, k, whole, whole, zz).wait_send()
    if GATHER:
        for k, whole in [(13, gz), (14, omr), (15, an_o.at[:, pl.ds(0, 2 * len(GATHER) * 128)])]:
            remote(0, k, whole, whole, zz).wait_send()


def hand_on(a, b, c, d, a_o, b_o, c_o, d_o, sem):
    copies = [pltpu.make_async_copy(p, o, sem.at[i]) for i, (p, o) in enumerate([(a, a_o), (b, b_o), (c, c_o), (d, d_o)])]
    for c in copies:
        c.start()
    for c in copies:
        c.wait()


def on_device(*args):
    V = pltpu.VMEM
    anyspace = pl.BlockSpec(memory_space=pl.ANY)
    shapes = tuple(jax.ShapeDtypeStruct(s, F32) for s in [(1, 16, 8192), (1, 16, 8192), (16, 1024), (16, 8192)])
    outs = pl.pallas_call(
        kernel,
        out_shape=tuple(V(s.shape, F32) for s in shapes),
        in_specs=[anyspace] * 8,
        out_specs=[pl.BlockSpec(memory_space=V)] * 4,
        scratch_shapes=[
            V((512, 512), jnp.bfloat16), V((512, 512), jnp.bfloat16), V((8, 512, W), jnp.bfloat16),
            V((16, 8192), F32), V((16, 8192), F32), V((16, 8192), F32), V((16, 8192), F32), V((16, 1024), F32),
            V((512, 512), jnp.bfloat16), V((16, 4, 4, 2, 8, W), F32),
            V((12, 2, 4, 2, 8, W), F32), V((12, 2, 2, 2, 8, W), F32), V((12, 2, 2, 8, W), F32), V((12, 2, 8, W), F32),
            V((12, 8, W), F32),
            V((4, 4, 4, 8, W), F32), V((4, 2, 4, 8, W), F32), V((4, 2, 2, 8, W), F32), V((4, 2, 8, W), F32),
            V((4, 2, 8, W // 2), F32),
            V((8, 2, 4, 16, 128), F32), V((8, 4, 16, 128), F32), V((8, 3, 16, 128), F32),
            V((max(len(GATHER), 1), 3, 4, 8, 128), F32), V((max(len(GATHER), 1), 3, 8, 128), F32),
            pltpu.SemaphoreType.DMA((CLASSES,)), pltpu.SemaphoreType.DMA((N_RECV,)),
            pltpu.SemaphoreType.DMA((15,)),
        ],
        compiler_params=pltpu.CompilerParams(
            collective_id=0, has_side_effects=True, vmem_limit_bytes=58 * 2**20
        ),
        cost_estimate=pl.CostEstimate(flops=4300000000, bytes_accessed=13000000, transcendentals=400000),
        name="round",
    )(*args)
    return pl.pallas_call(
        hand_on,
        out_shape=shapes,
        in_specs=[pl.BlockSpec(memory_space=V)] * 4,
        out_specs=[anyspace] * 4,
        scratch_shapes=[pltpu.SemaphoreType.DMA((4,))],
        name="hand_on",
    )(*[pltpu.with_memory_space_constraint(o, V) for o in outs])


def solution(mesh):
    rows = P("island", "fsdp", None)
    return jax.shard_map(
        on_device,
        mesh=mesh,
        in_specs=(rows,) * 6 + (P("fsdp", None), P("fsdp", "island")),
        out_specs=(rows, rows, P("fsdp", "island"), P("fsdp", None)),
        check_vma=False,
    )
```

```python
import functools

import jax
import jax.numpy as jnp
from jax import lax
from jax.experimental import pallas as pl
from jax.experimental.pallas import tpu as pltpu
from jax.sharding import PartitionSpec as P

MESH = pl.DeviceIdType.MESH
STEP = 100
F32 = jnp.float32
W = 1024
ORDER = [
    (0, 2), (0, 8), (0, 15), (0, 9), (0, 3), (0, 0), (1, 2), (0, 13), (1, 8), (0, 11), (1, 3), (1, 9), (1, 15),
    (1, 0), (0, 12), (2, 8), (1, 11), (2, 2), (2, 3), (2, 9), (1, 13), (2, 15), (2, 0), (3, 8), (0, 14), (0, 7),
    (3, 9), (0, 5), (2, 11), (2, 13), (3, 2), (3, 3), (4, 8), (0, 10), (4, 9), (3, 15), (0, 1), (3, 0), (1, 5),
    (1, 12), (1, 7), (3, 11), (3, 13), (4, 2), (4, 15), (4, 3), (0, 6), (0, 4), (1, 1), (1, 10), (1, 14), (5, 8),
    (4, 0), (5, 9), (5, 2), (5, 3), (6, 0), (2, 5), (6, 1), (5, 0), (2, 7), (6, 2), (4, 13), (2, 12), (6, 9), (4, 11),
    (5, 15), (1, 6), (7, 0), (6, 6), (1, 4), (5, 11), (7, 1), (7, 2), (7, 9), (6, 8), (2, 10), (8, 0), (2, 14),
    (2, 1), (3, 7), (7, 6), (3, 5), (5, 13), (8, 9), (3, 12), (7, 8), (6, 4), (2, 6), (2, 4), (3, 10), (3, 14),
    (3, 1), (8, 8), (4, 7), (7, 4), (3, 6), (4, 12), (5, 5), (3, 4), (4, 14), (5, 10), (6, 14), (5, 7), (4, 6),
    (5, 12), (6, 7), (5, 1), (6, 12), (5, 14), (5, 4), (6, 3), (6, 10), (5, 6), (6, 5), (6, 13), (7, 14), (6, 11),
    (7, 7), (7, 12), (7, 3), (7, 10), (7, 5), (7, 13), (8, 14), (7, 11), (8, 7), (8, 12), (8, 3), (8, 10), (8, 5),
    (8, 13),
]
GROUPS = [(4, None), (1, 0), (1, 1), (6, 0), (6, 1), (7, 0), (7, 1), (5, 0), (5, 1), (0, 0), (0, 1), (3, 0), (3, 1), (2, 0), (2, 1)]
DIRECT = [2, 4, 11]
SLANTED = [1, 4, 5, 10]
GATHER = [1, 6]
PER = 5
N_RECV = 16 * PER + 3 * len(GROUPS) + 1
CLASSES = 16

def kernel(
    gate, up, og, iw, fm, sm, an, om, fn_o, sn_o, mn_o, an_o,
    gv, uv, ov, iwv, fmv, smv, anv, omv,
    hb, T, L1, S1, L2, S2, LZ, CZ, CL1, CS1, CL2, CS2, dep, depc, hz, gz, omr,
    ssem, rsem, lsem,
):
    isl = lax.axis_index("island")
    f = lax.axis_index("fsdp")
    zh, core = isl // 2, isl % 2
    x, y, z = f // 8, (f // 2) % 4, f % 2

    def dev(x, y, z):
        return (isl, (x * 4 + y) * 2 + z)

    xp, xm = dev((x + 1) % 4, y, z), dev((x + 3) % 4, y, z)
    yp, ym = dev(x, (y + 1) % 4, z), dev(x, (y + 3) % 4, z)
    zz = dev(x, y, 1 - z)
    xpz, xmz = dev((x + 1) % 4, y, 1 - z), dev((x + 3) % 4, y, 1 - z)
    ypz, ymz = dev(x, (y + 1) % 4, 1 - z), dev(x, (y + 3) % 4, 1 - z)

    def island(rc, rz):
        return ((zh + rz) % 4) * 2 + (core + rc) % 2

    others = [(1, 0), (0, 1), (0, 2), (0, 3), (1, 1), (1, 2), (1, 3)]

    first = [pltpu.make_async_copy(gate.at[0], gv, lsem.at[0]), pltpu.make_async_copy(up.at[0], uv, lsem.at[1])]
    for c in first:
        c.start()

    def load_unit(u):
        def body(j, _):
            pltpu.make_async_copy(
                og.at[0, :, pl.ds(pl.multiple_of(j * 1024 + u * 128, 128), 128)],
                ov.at[u, :, pl.ds(pl.multiple_of(j * 128, 128), 128)],
                lsem.at[7 + u],
            ).start()
            return 0

        lax.fori_loop(0, 8, body, 0)

    used = []
    for s, i in ORDER:
        if s == 0 and i // 2 not in used:
            used.append(i // 2)
    for u in used[:2]:
        load_unit(u)
    state = [
        pltpu.make_async_copy(src, dst, lsem.at[2 + i])
        for i, (src, dst) in enumerate([(iw.at[0], iwv), (fm.at[0], fmv), (sm.at[0], smv), (an, anv), (om, omv)])
    ]
    barrier = pltpu.get_barrier_semaphore()
    peers = [xp, xm, yp, ym, zz]
    if any(c < 6 for c in SLANTED):
        peers += [ypz, ymz]
    if any(6 <= c < 12 for c in SLANTED):
        peers += [xpz, xmz]
    peers += [(island(rc, rz), f) for rc, rz in others]
    for d in peers:
        pl.semaphore_signal(barrier, inc=1, device_id=d, device_id_type=MESH)

    i = lax.broadcasted_iota(jnp.int32, (512, 512), 0)
    src = ((x + i // 64) % 4) * 128 + ((y + i // 16) % 4) * 32 + ((z + i // 8) % 2) * 16 + (i // 256) * 8 + i % 8
    pick = (src == lax.broadcasted_iota(jnp.int32, (512, 512), 1)).astype(F32).astype(jnp.bfloat16)
    for c in first:
        c.wait()

    for t in range(4):
        rows = slice(128 * t, 128 * t + 128)
        v = gv[rows, :].astype(F32)
        h = (v / (1.0 + jnp.exp(-v)) * uv[rows, :].astype(F32)).astype(jnp.bfloat16)
        hb[:, rows] = lax.dot_general(pick, h, (((1,), (1,)), ((), ())), preferred_element_type=F32).astype(jnp.bfloat16)
    pl.semaphore_wait(barrier, len(peers))

    def remote(n, k, src, dst, to):
        return pltpu.make_async_remote_copy(
            src_ref=src, dst_ref=dst, send_sem=ssem.at[k], recv_sem=rsem.at[n], device_id=to, device_id_type=MESH
        )

    def send(n, k, src, dst, to):
        remote(n, k, src, dst, to).start()

    def arrived(n, whole):
        remote(n, 0, whole, whole, zz).wait_recv()

    def add(dst, *srcs):
        n = dst.shape[0]
        if len(dst.shape) == 2:
            dst[...] = sum([s[...] for s in srcs], dst[...])
            return

        def body(i, _):
            dst[i] = sum([s[i] for s in srcs], dst[i])
            return 0

        lax.fori_loop(0, n, body, 0)

    def matmul(c):
        u, h = c // 2, c % 2

        def body(t, _):
            cols = pl.ds(pl.multiple_of(t * 256, 256), 256)
            r = lax.dot_general(
                hb[256 * h : 256 * h + 256, :], ov[u, :, cols], (((1,), (0,)), ((), ())), preferred_element_type=F32
            )
            T[c, :, :, :, :, cols] = r.astype(jnp.bfloat16).astype(F32).reshape(4, 4, 2, 8, 256)
            return 0

        lax.fori_loop(0, W // 256, body, 0)

    def blocks(c, ks):
        u, h = c // 2, c % 2
        if c < 6:
            parts = [hb[256 * h + 64 * k : 256 * h + 64 * k + 64, :] for k in ks]
        else:
            parts = [hb[256 * h + 64 * a + 16 * k : 256 * h + 64 * a + 16 * k + 16, :] for k in ks for a in range(4)]
        left = jnp.concatenate(parts, axis=0)

        def body(t, _):
            cols = pl.ds(pl.multiple_of(t * 256, 256), 256)
            r = lax.dot_general(left, ov[u, :, cols], (((1,), (0,)), ((), ())), preferred_element_type=F32)
            r = r.astype(jnp.bfloat16).astype(F32).reshape(len(ks), 4, 2, 8, 256)
            for n, k in enumerate(ks):
                if c < 6:
                    T[c, k, :, :, :, cols] = r[n]
                else:
                    T[c, :, k, :, :, cols] = r[n]
            return 0

        lax.fori_loop(0, W // 256, body, 0)

    def ring_far(n, k, blk, one, two, ones, twos, plus, minus, plus1, minus1):
        send(n, k, blk(2, 0), one(0), plus)
        send(n, k, blk(2, 1), one(1), minus)

    def ring_near(n, k, blk, one, two, ones, twos, plus, minus, plus1, minus1):
        send(n + 1, k + 1, blk(1, 1), two(0, 1), plus1)
        send(n + 1, k + 1, blk(3, 0), two(1, 0), minus)

    def ring_raw(*ring):
        ring_far(*ring)
        ring_near(*ring)

    def ring_mid(n, k, blk, one, two, ones, twos, plus, minus, plus1, minus1):
        arrived(n, ones)
        add(blk(1, 0), one(0))
        send(n + 1, k + 1, blk(1, 0), two(0, 0), plus)
        add(blk(3, 1), one(1))
        send(n + 1, k + 1, blk(3, 1), two(1, 1), minus1)

    def ring_end(n, k, blk, one, two, ones, twos, plus, minus, plus1, minus1):
        arrived(n + 1, twos)
        add(blk(0), two(0), two(1))

    def rings(c):
        t = T.at[c]
        two = pl.ds(0, 2), pl.ds(2, 2)
        if c < 12:
            if c < 6:
                b1 = lambda k, half=None: t.at[k] if half is None else t.at[k, two[half]]
                b2 = lambda k, half=None: t.at[0, k] if half is None else t.at[0, k, half]
            else:
                b1 = lambda k, half=None: t.at[:, k] if half is None else t.at[two[half], k]
                b2 = lambda k, half=None: t.at[k, 0] if half is None else t.at[k, 0, half]
            l1 = lambda d, half=None: L1.at[c, d] if half is None else L1.at[c, d, two[half]]
            l2 = lambda d, half=None: L2.at[c, d] if half is None else L2.at[c, d, half]
            s1, s2 = (lambda d: S1.at[c, d]), (lambda d: S2.at[c, d])
            w1, w2 = (S1.at[c], L1.at[c]), (S2.at[c], L2.at[c])
            k = 0
        else:
            i = c - 12
            part = pl.ds(0, 512), pl.ds(512, 512)
            if c < 14:
                b1 = lambda k, half=None: t.at[k, :, 0] if half is None else t.at[k, two[half], 0]
                b2 = lambda k, half=None: t.at[0, k, 0] if half is None else t.at[0, k, 0, :, part[half]]
            else:
                b1 = lambda k, half=None: t.at[:, k, 0] if half is None else t.at[two[half], k, 0]
                b2 = lambda k, half=None: t.at[k, 0, 0] if half is None else t.at[k, 0, 0, :, part[half]]
            l1 = lambda d, half=None: CL1.at[i, d] if half is None else CL1.at[i, d, two[half]]
            l2 = lambda d, half=None: CL2.at[i, d] if half is None else CL2.at[i, d, :, part[half]]
            s1, s2 = (lambda d: CS1.at[i, d]), (lambda d: CS2.at[i, d])
            w1, w2 = (CS1.at[i], CL1.at[i]), (CS2.at[i], CL2.at[i])
            k = 5
        along_x, along_y = (xp, xm), (yp, ym)
        d1, d2 = (along_x, along_y) if c < 6 or 12 <= c < 14 else (along_y, along_x)
        n = c * PER
        e2 = d2
        if c in SLANTED:
            e2 = (ypz, ymz) if c < 6 else (xpz, xmz)
        return (n, k, b1, s1, l1) + w1 + d1 + d1, (n + 2, k + 2, b2, s2, l2) + w2 + d2 + e2

    def update(c):
        u, h = c // 2, c % 2
        rows = pl.ds(8 * h, 8)
        first_fix = 1.0 - 0.9**STEP
        second_fix = 1.0 - 0.95**STEP

        def body(r, _):
            rc, rz = r // 4, r % 4
            j = island(rc, rz)
            cols = pl.ds(pl.multiple_of(j * 1024 + u * 128, 128), 128)
            g = T[c, 0, 0, 0, :, pl.ds(pl.multiple_of(j * 128, 128), 128)]
            first_next = 0.9 * fmv[rows, cols] + 0.1 * g
            second_next = 0.95 * smv[rows, cols] + 0.05 * g * g
            fn_o[0, rows, cols] = first_next
            sn_o[0, rows, cols] = second_next
            upd = first_next / first_fix / (jnp.sqrt(second_next / second_fix) + 1e-08)
            w = iwv[rows, cols]
            dep[u, rc, rz, rows, :] = anv[rows, cols] - (w - 0.05 * (upd + 0.4 * w))
            return 0

        lax.fori_loop(0, 8, body, 0, unroll=True)

    updated = [0]

    def finish_chunk(c):
        u = c // 2
        if updated[0] == 0:
            for s in state:
                s.wait()
            for k, g in enumerate(GATHER):
                u, rows, n = group(g)
                for rz in (2, 1, 3):
                    send(n + 2, 14, omv.at[rows, pl.ds(128 * u, 128)], omr.at[k, rz - 1], (island(0, rz), f))
        update(c)
        updated[0] += 1
        done.add(c)
        for g, (u, h) in enumerate(GROUPS):
            if c // 2 == u and (h == c % 2 or h is None and c ^ 1 in done):
                u, rows, n = group(g)
                send(n, 10, dep.at[u, 1, :, rows], depc.at[u, :, rows], (island(1, 0), f))

    done = set()
    own = isl * 1024

    def group(g):
        u, h = GROUPS[g]
        return u, pl.ds(0, 16) if h is None else pl.ds(8 * h, 8), 16 * PER + 3 * g

    def island_one(g):
        u, rows, n = group(g)
        arrived(n, depc.at[u, :, rows])
        add(dep.at[u, 0, :, rows], depc.at[u, :, rows])
        if g in GATHER:
            for rz in (2, 1, 3):
                send(n + 1, 13, dep.at[u, 0, :, rows], gz.at[GATHER.index(g), rz - 1], (island(0, rz), f))
            return
        for rz in (2, 1, 3):
            send(n + 1, 11, dep.at[u, 0, rz, rows], hz.at[u, rz - 1, rows], (island(0, rz), f))

    def gathered(g):
        u, rows, n = group(g)
        k = GATHER.index(g)
        arrived(n + 2, omr.at[k])
        arrived(n + 1, gz.at[k])

        def result(r, old):
            pseudo = ((dep[u, 0, r, rows] + gz[k, 1, (r + 2) % 4]) + (gz[k, 0, (r + 1) % 4] + gz[k, 2, (r + 3) % 4])) / 8
            momentum = 0.9 * old + pseudo
            out = pl.ds(pl.multiple_of(island(0, r) * 1024 + u * 128, 128), 128)
            an_o[rows, out] = anv[rows, out] - 0.7 * (pseudo + 0.9 * momentum)
            send(N_RECV - 1, 15, an_o.at[rows, out], an_o.at[rows, out], (island(1, 0), f))
            return momentum

        cols = pl.ds(128 * u, 128)
        mn_o[rows, cols] = result(0, omv[rows, cols])
        for r in (1, 2, 3):
            result(r, omr[k, 3 - r])

    def island_two(g):
        if g in GATHER:
            gathered(g)
            return
        u, rows, n = group(g)
        arrived(n + 1, hz.at[u, :, rows])
        cols = pl.ds(128 * u, 128)
        pseudo = (dep[u, 0, 0, rows] + hz[u, 0, rows] + hz[u, 1, rows] + hz[u, 2, rows]) / 8
        momentum = 0.9 * omv[rows, cols] + pseudo
        mn_o[rows, cols] = momentum
        out = pl.ds(pl.multiple_of(own + u * 128, 128), 128)
        an_o[rows, out] = anv[rows, out] - 0.7 * (pseudo + 0.9 * momentum)
        res = an_o.at[rows, out]
        for rz in (2, 1, 3):
            send(n + 2, 12, res, res, (island(0, rz), f))
            if g in DIRECT:
                send(N_RECV - 1, 12, res, res, (island(1, rz), f))
        send(N_RECV - 1, 12, res, res, (island(1, 0), f))

    def island_three(g):
        u, rows, n = group(g)
        arrived(n + 2, an_o.at[rows, pl.ds(0, 3 * 128)])
        if g not in DIRECT:
            for rz in (1, 2, 3):
                out = pl.ds(pl.multiple_of(island(0, rz) * 1024 + u * 128, 128), 128)
                send(N_RECV - 1, 12, an_o.at[rows, out], an_o.at[rows, out], (island(1, 0), f))

    def fetched(u):
        used.remove(u)
        if len(used) > 1:
            load_unit(used[1])
        if len(used) == 4:
            for c in state:
                c.start()
        pltpu.make_async_copy(og.at[0, :, pl.ds(0, W)], ov.at[u], lsem.at[7 + u]).wait()

    early = [i for s, i in ORDER if s == 0][:2]
    if max(early) >= 12 or early[0] // 2 == early[1] // 2:
        early = []

    for s, i in ORDER:
        if s == 6:
            island_one(i)
            continue
        if s == 7:
            island_two(i)
            continue
        if s == 8:
            island_three(i)
            continue
        r1, r2 = rings(i)
        if s == 0 and i in early:
            if i == early[0]:
                for c in early:
                    fetched(c // 2)
                    blocks(c, [2])
                    ring_far(*rings(c)[0])
                for c in early:
                    blocks(c, [1, 3, 0])
                    ring_near(*rings(c)[0])
            continue
        if s == 0:
            if i // 2 in used:
                fetched(i // 2)
            matmul(i)
        if i < 12:
            if s == 0:
                ring_raw(*r1)
            elif s == 1:
                ring_mid(*r1)
            elif s == 2:
                ring_end(*r1)
                ring_raw(*r2)
                if i in SLANTED:
                    send(i * PER + 4, 4, T.at[i, 0, 0, 1], LZ.at[i], zz)
            elif s == 3:
                ring_mid(*r2)
            elif s == 4:
                ring_end(*r2)
                send(i * PER + 4, 4, T.at[i, 0, 0, 1], LZ.at[i], zz)
            else:
                arrived(i * PER + 4, LZ.at[i])
                more = []
                if i in SLANTED:
                    arrived(i * PER + 3, L2.at[i])
                    more = [L2.at[i, d, k] for d in (0, 1) for k in (0, 1)]
                add(T.at[i, 0, 0, 0], LZ.at[i], *more)
                finish_chunk(i)
        else:
            if s == 0:
                send(i * PER + 4, 9, T.at[i, :, :, 1], CZ.at[i - 12], zz)
            elif s == 1:
                arrived(i * PER + 4, CZ.at[i - 12])
                for k in range(4):
                    add(T.at[i, k, :, 0], CZ.at[i - 12, k])
                ring_raw(*r1)
            elif s == 2:
                ring_mid(*r1)
            elif s == 3:
                ring_end(*r1)
                ring_raw(*r2)
            elif s == 4:
                ring_mid(*r2)
            else:
                ring_end(*r2)
                finish_chunk(i)

    for g in DIRECT:
        island_three(g)
    arrived(N_RECV - 1, an_o.at[:, pl.ds(0, 4 * 1024)])
    plain = 16 - len(GATHER)
    for k, whole in [
        (0, S1), (1, L1), (2, S2), (3, L2), (4, LZ), (5, CS1), (6, CL1), (7, CS2), (8, CL2), (9, CZ), (10, depc),
        (11, hz.at[pl.ds(0, plain // 2)]), (12, an_o.at[:, pl.ds(0, 7 * plain // 2 * 128)]),
    ]:
        remote(0, k, whole, whole, zz).wait_send()
    if GATHER:
        for k, whole in [(13, gz), (14, omr), (15, an_o.at[:, pl.ds(0, 2 * len(GATHER) * 128)])]:
            remote(0, k, whole, whole, zz).wait_send()


def hand_on(a, b, c, d, a_o, b_o, c_o, d_o, sem):
    copies = [pltpu.make_async_copy(p, o, sem.at[i]) for i, (p, o) in enumerate([(a, a_o), (b, b_o), (c, c_o), (d, d_o)])]
    for c in copies:
        c.start()
    for c in copies:
        c.wait()


def on_device(*args):
    V = pltpu.VMEM
    anyspace = pl.BlockSpec(memory_space=pl.ANY)
    shapes = tuple(jax.ShapeDtypeStruct(s, F32) for s in [(1, 16, 8192), (1, 16, 8192), (16, 1024), (16, 8192)])
    outs = pl.pallas_call(
        kernel,
        out_shape=tuple(V(s.shape, F32) for s in shapes),
        in_specs=[anyspace] * 8,
        out_specs=[pl.BlockSpec(memory_space=V)] * 4,
        scratch_shapes=[
            V((512, 512), jnp.bfloat16), V((512, 512), jnp.bfloat16), V((8, 512, W), jnp.bfloat16),
            V((16, 8192), F32), V((16, 8192), F32), V((16, 8192), F32), V((16, 8192), F32), V((16, 1024), F32),
            V((512, 512), jnp.bfloat16), V((16, 4, 4, 2, 8, W), F32),
            V((12, 2, 4, 2, 8, W), F32), V((12, 2, 2, 2, 8, W), F32), V((12, 2, 2, 8, W), F32), V((12, 2, 8, W), F32),
            V((12, 8, W), F32),
            V((4, 4, 4, 8, W), F32), V((4, 2, 4, 8, W), F32), V((4, 2, 2, 8, W), F32), V((4, 2, 8, W), F32),
            V((4, 2, 8, W // 2), F32),
            V((8, 2, 4, 16, 128), F32), V((8, 4, 16, 128), F32), V((8, 3, 16, 128), F32),
            V((max(len(GATHER), 1), 3, 4, 8, 128), F32), V((max(len(GATHER), 1), 3, 8, 128), F32),
            pltpu.SemaphoreType.DMA((CLASSES,)), pltpu.SemaphoreType.DMA((N_RECV,)),
            pltpu.SemaphoreType.DMA((15,)),
        ],
        compiler_params=pltpu.CompilerParams(
            collective_id=0, has_side_effects=True, vmem_limit_bytes=58 * 2**20
        ),
        cost_estimate=pl.CostEstimate(flops=4300000000, bytes_accessed=13000000, transcendentals=400000),
        name="round",
    )(*args)
    return pl.pallas_call(
        hand_on,
        out_shape=shapes,
        in_specs=[pl.BlockSpec(memory_space=V)] * 4,
        out_specs=[anyspace] * 4,
        scratch_shapes=[pltpu.SemaphoreType.DMA((4,))],
        name="hand_on",
    )(*[pltpu.with_memory_space_constraint(o, V) for o in outs])


def solution(mesh):
    rows = P("island", "fsdp", None)
    return jax.shard_map(
        on_device,
        mesh=mesh,
        in_specs=(rows,) * 6 + (P("fsdp", None), P("fsdp", "island")),
        out_specs=(rows, rows, P("fsdp", "island"), P("fsdp", None)),
        check_vma=False,
    )
```
